256 devices in a mesh: blk: 256 (over y, z, x, core).
Axes of the slice: x: 4, y: 4, z: 8, core: 2. Of those that a mesh axis runs over, the one named last changes fastest.
Arguments:
- features: bfloat16 [131072, 8192], P('blk'), may hold values from -600 to 600
- sources: int32 [131072], P('blk'), may hold values from 0 to 3
Outputs:
- similarity: bfloat16 [131072, 6, 512], P('blk')
The draws below stay inside these ranges and needn't reach their ends.
All inputs are finite; a program needn't handle non-finite values.
Results may differ from the reference program's by a relative error of at most 0.0057.
Values may be sent and summed in bfloat16 or wider, within the bound.
No kernel may reach another device: no remote copies, remote signals or barrier semaphores. Data moves between devices by JAX's collectives and lax.ppermute only.
A program may use at most 128 MiB of HBM per device.

```python
import jax
import jax.numpy as jnp
from jax import lax

B = 512
P_SIZE = 8192
ROUNDS = 3
SOURCES = 4
TOTAL = 131072
N_BLK = 256


def draw_features(key, part):
    key = jax.random.fold_in(key, 11)
    key_shared, key_noise, key_scale, key_coef, key_cols = jax.random.split(key, 5)
    shared = jnp.clip(jax.random.normal(key_shared, (P_SIZE,), jnp.float32), -5.0, 5.0)
    columns = jnp.exp(jax.random.uniform(key_cols, (P_SIZE,), jnp.float32) * jnp.log(10.0))
    noise = jnp.clip(jax.random.normal(key_noise, (TOTAL, P_SIZE), jnp.float32), -5.0, 5.0)
    scales = jnp.exp(jax.random.uniform(key_scale, (TOTAL,), jnp.float32) * jnp.log(10.0))
    coefs = jax.random.uniform(key_coef, (TOTAL,), jnp.float32, 0.0, 0.1)
    values = scales[:, None] * columns[None, :] * (noise + coefs[:, None] * shared[None, :])
    return values.astype(jnp.bfloat16)


def set_ends(entries, own_key, low, high):
    shape = entries.shape
    index_at = [jax.random.randint(jax.random.fold_in(own_key, axis), (), 0, shape[axis]) for axis in range(len(shape))]
    entries = entries.at[tuple(index_at)].set(low)
    longest = shape.index(max(shape))
    index_at[longest] = (index_at[longest] + 1) % shape[longest]
    return entries.at[tuple(index_at)].set(high)


def setup_inputs(seed: int = 0) -> dict:
    streams_of = jax.random.split(jax.random.key(seed), 3)
    features = draw_features(jax.random.fold_in(streams_of[2], 71), 0)
    sources = set_ends(jax.random.randint(streams_of[1], (TOTAL,), 0, SOURCES), jax.random.fold_in(streams_of[1], 1), 0, SOURCES - 1).astype(jnp.int32)
    return dict(features=features, sources=sources)


def reference(features, sources):
    squares = lax.optimization_barrier(jnp.sum(jnp.square(features.astype(jnp.float32)), axis=1, keepdims=True))
    unit = (features.astype(jnp.float32) / jnp.sqrt(squares + 1e-06)).astype(jnp.bfloat16)
    blocks = unit.reshape(N_BLK, B, P_SIZE)
    labels = sources.reshape(N_BLK, B)
    slots = []
    for step in range(ROUNDS):
        dist = N_BLK // 2 - ROUNDS + step

        def one_tile(index):
            other = (index + dist) % N_BLK
            left = lax.dynamic_index_in_dim(blocks, index, 0, False)
            right = lax.dynamic_index_in_dim(blocks, other, 0, False)
            tile = lax.dot_general(left, right, (((1,), (1,)), ((), ())), preferred_element_type=jnp.float32)
            same = lax.dynamic_index_in_dim(labels, index, 0, False)[:, None] == lax.dynamic_index_in_dim(labels, other, 0, False)[None, :]
            return jnp.where(same, jnp.float32(0.0), tile).astype(jnp.bfloat16)
        forward = lax.map(one_tile, jnp.arange(N_BLK, dtype=jnp.int32))
        backward = jnp.swapaxes(jnp.roll(forward, dist, axis=0), 1, 2)
        slots.append(forward)
        slots.append(backward)
    stacked = jnp.stack(slots, axis=2)
    return stacked.reshape(N_BLK * B, 2 * ROUNDS, B)
```

```python
import jax
import jax.numpy as jnp
from jax import lax
from jax.experimental import pallas as pl
from jax.experimental.pallas import tpu as pltpu
from jax.sharding import PartitionSpec as P

N = 256
SEAM = 128
B = 512
HALF = 4096
TAG = 128
WIDE = HALF + TAG
KSTEP = 1024
ROWS = 64
MIB = 1024 * 1024


def send(block, target, only=None):
    pairs = [(i, target(i) % N) for i in range(N) if only is None or only(i)]
    return lax.ppermute(block, "blk", pairs)


def unit_kernel(info, x_ref, tag_ref, keep_ref, other_ref, ahead_ref):
    x = x_ref[...].astype(jnp.float32)
    squares = jnp.sum(x * x, axis=1, keepdims=True)
    unit = (x * (1.0 / jnp.sqrt(squares + 1e-06))).astype(jnp.bfloat16)
    low, high = unit[:, :HALF], unit[:, HALF:]
    tag = tag_ref[...]

    def put(ref, half):
        @pl.when(half == 0)
        def _():
            ref[:, :HALF] = low

        @pl.when(half != 0)
        def _():
            ref[:, :HALF] = high

        ref[:, HALF:] = tag

    put(keep_ref, info[0])
    put(other_ref, 1 - info[0])
    put(ahead_ref, info[1])


def make_units(features, tags, own_half, ahead_half):
    out = jax.ShapeDtypeStruct((B, WIDE), jnp.bfloat16)
    spec = pl.BlockSpec((ROWS, WIDE), lambda r, info: (r, 0))
    return pl.pallas_call(
        unit_kernel,
        out_shape=(out, out, out),
        grid_spec=pltpu.PrefetchScalarGridSpec(
            num_scalar_prefetch=1,
            grid=(B // ROWS,),
            in_specs=[
                pl.BlockSpec((ROWS, 2 * HALF), lambda r, info: (r, 0)),
                pl.BlockSpec((ROWS, TAG), lambda r, info: (r, 0)),
            ],
            out_specs=(spec, spec, spec),
        ),
        compiler_params=pltpu.CompilerParams(vmem_limit_bytes=40 * MIB),
        cost_estimate=pl.CostEstimate(flops=12 * B * HALF, bytes_accessed=20 * MIB, transcendentals=B),
        name="units",
    )(jnp.stack([own_half, ahead_half]).astype(jnp.int32), features, tags)


def tiles(plans, rows, blocks, choices):
    count = len(plans)
    used_rows, used_blocks = len(rows), len(blocks)

    def kernel(info, *refs):
        row_refs = refs[:used_rows]
        block_refs = refs[used_rows : used_rows + used_blocks]
        refs = refs[used_rows + used_blocks :]
        row_tags = refs[:used_rows]
        block_tags = refs[used_rows : used_rows + used_blocks]
        refs = refs[used_rows + used_blocks :]
        out_ref, turned = refs[0], refs[1 : 1 + count]
        total = refs[1 + count]
        step = pl.program_id(0)

        def each(work):
            for t, options in enumerate(plans):
                if len(options) == 1:
                    work(t, options[0][0], options[0][1])
                    continue
                for c, (a, b) in enumerate(options):
                    @pl.when(info[t] == c)
                    def _(t=t, a=a, b=b):
                        work(t, a, b)

        def add(t, a, b):
            part = lax.dot_general(
                row_refs[a][...], block_refs[b][...], (((1,), (1,)), ((), ())), preferred_element_type=jnp.float32
            )

            @pl.when(step == 0)
            def _():
                total[t] = part

            @pl.when(step > 0)
            def _():
                total[t] += part

        each(add)

        @pl.when(step == HALF // KSTEP - 1)
        def _():
            def finish(t, a, b):
                same = lax.dot_general(
                    row_tags[a][...], block_tags[b][...], (((1,), (1,)), ((), ())), preferred_element_type=jnp.float32
                )
                tile = jnp.where(same > 0.5, jnp.float32(0.0), total[t])
                out_ref[t] = tile.astype(jnp.bfloat16)
                turned[t][...] = tile.T.astype(jnp.bfloat16)

            each(finish)

    wide = pl.BlockSpec((B, KSTEP), lambda k, info: (0, k))
    tag = pl.BlockSpec((B, TAG), lambda k, info: (0, HALF // TAG))
    arrays = list(rows) + list(blocks)
    one = jax.ShapeDtypeStruct((B, B), jnp.bfloat16)
    return pl.pallas_call(
        kernel,
        out_shape=(jax.ShapeDtypeStruct((count, B, B), jnp.bfloat16),) + (one,) * count,
        grid_spec=pltpu.PrefetchScalarGridSpec(
            num_scalar_prefetch=1,
            grid=(HALF // KSTEP,),
            in_specs=[wide] * len(arrays) + [tag] * len(arrays),
            out_specs=(pl.BlockSpec((count, B, B), lambda k, info: (0, 0, 0)),)
            + (pl.BlockSpec((B, B), lambda k, info: (0, 0)),) * count,
            scratch_shapes=[pltpu.VMEM((count, B, B), jnp.float32)],
        ),
        compiler_params=pltpu.CompilerParams(vmem_limit_bytes=48 * MIB),
        cost_estimate=pl.CostEstimate(
            flops=2 * count * B * B * HALF, bytes_accessed=4 * MIB * (len(arrays)), transcendentals=0
        ),
        name="tiles",
    )(jnp.stack(choices).astype(jnp.int32), *arrays, *arrays)


def sum_kernel(slots, first, second, third, *refs):
    turned, out_ref = refs[:6], refs[6]
    straight = [first[0], first[1], first[2], second[0], second[1], third[0]]
    for k, back in enumerate((0, 2, 1, 4, 3, 5)):
        both = straight[k].astype(jnp.float32) + turned[back][...].astype(jnp.float32)
        out_ref[slots[k]] = both.astype(jnp.bfloat16)


def add_up(slots, straight, turned):
    whole = pl.BlockSpec(memory_space=pltpu.VMEM)
    return pl.pallas_call(
        sum_kernel,
        out_shape=jax.ShapeDtypeStruct((6, B, B), jnp.bfloat16),
        in_specs=[pl.BlockSpec(memory_space=pltpu.SMEM)] + [whole] * 9,
        out_specs=whole,
        compiler_params=pltpu.CompilerParams(vmem_limit_bytes=40 * MIB),
        cost_estimate=pl.CostEstimate(flops=6 * B * B, bytes_accessed=9 * MIB, transcendentals=0),
        name="add_up",
    )(slots, *straight, *turned)


def local(features, sources):
    me = lax.axis_index("blk")
    odd = me % 2
    place = me % SEAM
    own_half = me // SEAM
    tags = (sources[:, None] == jnp.arange(TAG, dtype=sources.dtype)[None, :]).astype(jnp.bfloat16)
    keep, other, ahead = make_units(features, tags, own_half, ((me - 2) % N) // SEAM)

    opposite = send(other, lambda i: i + SEAM)
    second_half = send(keep, lambda i: i + SEAM, lambda i: i % SEAM < 3)
    after2 = send(ahead, lambda i: i - 2)
    before2 = send(keep, lambda i: i + 2)
    mate = send(keep, lambda i: i ^ 1)
    lone = send(other, lambda i: i - 3, lambda i: i % SEAM == 2)
    after_mate = send(after2, lambda i: i ^ 1)
    before_mate = send(before2, lambda i: i ^ 1)
    before3 = send(before2, lambda i: i + 1, lambda i: i % 2 == 1)
    after3 = send(after2, lambda i: i - 1, lambda i: i % 2 == 0 and i % SEAM != 0)

    zero = jnp.zeros((), jnp.int32)
    near, *near_turned = tiles(
        [[(0, 0)], [(0, 1)], [(0, 2), (1, 2)]],
        [opposite, second_half],
        [mate, after2, before2],
        [zero, zero, place < 2],
    )
    mid, *mid_turned = tiles(
        [[(0, 0)], [(0, 1), (1, 1)]], [opposite, second_half], [after_mate, before_mate], [zero, place < 2]
    )
    far_choice = jnp.where(odd == 1, jnp.where(place == SEAM - 1, 3, 2), jnp.where(place < 3, 1, 0))
    far, *far_turned = tiles(
        [[(0, 0), (1, 0), (0, 1), (0, 2)]], [opposite, second_half], [before3, after3, lone], [far_choice]
    )

    straight = [send(t, lambda i: i + SEAM) for t in (near, mid, far)]
    turned = [
        send(near_turned[0], lambda i: i ^ 1),
        send(near_turned[1], lambda i: i + 2),
        send(near_turned[2], lambda i: i - 2),
        send(mid_turned[0], lambda i: i + 1 if i % 2 else i + 3),
        send(mid_turned[1], lambda i: i - 3 if i % 2 else i - 1),
        send(far_turned[0], lambda i: i + 3 if i % 2 else i - 3),
    ]
    slots = jnp.where(odd == 1, jnp.array([4, 3, 2, 5, 0, 1], jnp.int32), jnp.array([5, 3, 2, 1, 4, 0], jnp.int32))
    return jnp.transpose(add_up(slots, straight, turned), (1, 0, 2))


def solution(mesh):
    return jax.shard_map(
        local,
        mesh=mesh,
        in_specs=(P("blk", None), P("blk")),
        out_specs=P("blk", None, None),
        check_vma=False,
    )
```

```python
import jax
import jax.numpy as jnp
from jax import lax
from jax.experimental import pallas as pl
from jax.experimental.pallas import tpu as pltpu
from jax.sharding import PartitionSpec as P

N = 256
SEAM = 128
SEAM_AT = 32
PLANE = 64
B = 512
HALF = 4096
TAG = 128
WIDE = HALF + TAG
NSTEP = 256
ROWS = 64
MIB = 1024 * 1024


def send(block, target, only=None):
    pairs = [(i, target(i) % N) for i in range(N) if only is None or only(i)]
    return lax.ppermute(block, "blk", pairs)


def hold(block, *others):
    return lax.optimization_barrier((block,) + others)[0]


def at(y, z, x, core):
    return ((y % 4 * 8 + z % 8) * 4 + x % 4) * 2 + core


def corner(i):
    spot = i % PLANE
    side = 1 if spot < 2 else 2 if spot >= PLANE - 2 else 0
    return i // PLANE, side, i % 2


DOWN = {(0, 0): (0, 0), (0, 1): (7, 0)}
UP = {(0, 0): (7, 3), (0, 1): (0, 3)}
SPLIT = 336


def border_routes(part):
    first, second = [], []
    for y in range(4):
        for core in range(2):
            for source, plane, via, goal in (
                (at(y, 0, 0, core), y - 1, DOWN, at(y - 1, 7, 3, core)),
                (at(y, 7, 3, core), y + 1, UP, at(y + 1, 0, 0, core)),
            ):
                if (part, core) in via:
                    middle = at(plane, *via[part, core], core)
                    first.append((source, middle))
                    second.append((middle, goal))
                else:
                    first.append((source, goal))
    return first, second


def unit_kernel(info, x_ref, tag_ref, keep_ref, other_ref, ahead_ref):
    x = x_ref[...].astype(jnp.float32)
    squares = jnp.sum(x * x, axis=1, keepdims=True)
    unit = (x * (1.0 / jnp.sqrt(squares + 1e-06))).astype(jnp.bfloat16)
    low, high = unit[:, :HALF], unit[:, HALF:]
    tag = tag_ref[...]

    def put(ref, half):
        @pl.when(half == 0)
        def _():
            ref[:, :HALF] = low

        @pl.when(half != 0)
        def _():
            ref[:, :HALF] = high

        ref[:, HALF:] = tag

    put(keep_ref, info[0])
    put(other_ref, 1 - info[0])
    put(ahead_ref, info[1])


def make_units(features, tags, own_half, ahead_half):
    out = jax.ShapeDtypeStruct((B, WIDE), jnp.bfloat16)
    spec = pl.BlockSpec((ROWS, WIDE), lambda r, info: (r, 0))
    return pl.pallas_call(
        unit_kernel,
        out_shape=(out, out, out),
        grid_spec=pltpu.PrefetchScalarGridSpec(
            num_scalar_prefetch=1,
            grid=(B // ROWS,),
            in_specs=[
                pl.BlockSpec((ROWS, 2 * HALF), lambda r, info: (r, 0)),
                pl.BlockSpec((ROWS, TAG), lambda r, info: (r, 0)),
            ],
            out_specs=(spec, spec, spec),
        ),
        compiler_params=pltpu.CompilerParams(vmem_limit_bytes=40 * MIB),
        cost_estimate=pl.CostEstimate(flops=12 * B * HALF, bytes_accessed=20 * MIB, transcendentals=B),
        name="units",
    )(jnp.stack([own_half, ahead_half]).astype(jnp.int32), features, tags)


def tiles(rows, blocks, row_choice, block_choice, seam_tiles, stacked=(), extra=None):
    count = len(blocks)
    used_rows = len(rows)
    flat = [array for entry in blocks for array in entry]
    alone = [t for t in range(count) if t not in stacked]
    lead = 0 if extra is None else 1

    def kernel(info, *refs):
        row_refs = refs[:used_rows]
        block_refs = []
        at_ref = used_rows
        for entry in blocks:
            block_refs.append(refs[at_ref : at_ref + len(entry)])
            at_ref += len(entry)
        if lead:
            extra_ref = refs[at_ref]
            at_ref += 1
        out_ref = refs[at_ref]
        turned = {t: refs[at_ref + 1 + k] for k, t in enumerate(alone)}
        at_ref += 1 + len(alone)
        if stacked:
            for k, t in enumerate(stacked):
                turned[t] = refs[at_ref].at[lead + k]
            stack_ref = refs[at_ref]
            at_ref += 1
        held_rows, held_blocks, row_sems, block_sems = refs[at_ref:]

        pltpu.make_async_copy(row_refs[0], held_rows.at[0], row_sems.at[0]).start()
        for t in range(count):
            for c, ref in enumerate(block_refs[t]):
                @pl.when(info[1 + t] == c)
                def _(t=t, ref=ref):
                    pltpu.make_async_copy(ref, held_blocks.at[t], block_sems.at[t]).start()
            if t == 0:
                for c in range(1, used_rows):
                    @pl.when(info[0] == c)
                    def _(c=c):
                        pltpu.make_async_copy(row_refs[c], held_rows.at[1], row_sems.at[1]).start()

        pltpu.make_async_copy(row_refs[0], held_rows.at[0], row_sems.at[0]).wait()
        if lead:
            stack_ref[0] = extra_ref[...]
        waited = False
        for t in range(count):
            which = 0
            if t in seam_tiles:
                if not waited:
                    @pl.when(info[0] > 0)
                    def _():
                        pltpu.make_async_copy(row_refs[0], held_rows.at[1], row_sems.at[1]).wait()
                    waited = True
                which = jnp.minimum(info[0], 1)
            pltpu.make_async_copy(block_refs[t][0], held_blocks.at[t], block_sems.at[t]).wait()

            def chunk(n, _, t=t, which=which):
                span = pl.ds(pl.multiple_of(n * NSTEP, NSTEP), NSTEP)
                over = (((1,), (1,)), ((), ()))
                tile = lax.dot_general(
                    held_rows[which, :, :HALF], held_blocks[t, span, :HALF], over, preferred_element_type=jnp.float32
                )
                same = lax.dot_general(
                    held_rows[which, :, HALF:], held_blocks[t, span, HALF:], over, preferred_element_type=jnp.float32
                )
                tile = jnp.where(same > 0.5, jnp.float32(0.0), tile)
                out_ref[t, :, span] = tile.astype(jnp.bfloat16)
                turned[t][span, :] = tile.T.astype(jnp.bfloat16)
                return 0

            lax.fori_loop(0, B // NSTEP, chunk, 0)

    one = jax.ShapeDtypeStruct((B, B), jnp.bfloat16)
    whole = pl.BlockSpec(memory_space=pltpu.VMEM)
    info = jnp.stack([row_choice] + list(block_choice)).astype(jnp.int32)
    outs = (jax.ShapeDtypeStruct((count, B, B), jnp.bfloat16),) + (one,) * len(alone)
    if stacked:
        outs += (jax.ShapeDtypeStruct((lead + len(stacked), B, B), jnp.bfloat16),)
    return pl.pallas_call(
        kernel,
        out_shape=outs,
        in_specs=[pl.BlockSpec(memory_space=pltpu.SMEM)]
        + [pl.BlockSpec(memory_space=pl.ANY)] * (used_rows + len(flat))
        + [whole] * lead,
        out_specs=(whole,) * len(outs),
        scratch_shapes=[
            pltpu.VMEM((2, B, WIDE), jnp.bfloat16),
            pltpu.VMEM((count, B, WIDE), jnp.bfloat16),
            pltpu.SemaphoreType.DMA((2,)),
            pltpu.SemaphoreType.DMA((count,)),
        ],
        compiler_params=pltpu.CompilerParams(vmem_limit_bytes=50 * MIB),
        cost_estimate=pl.CostEstimate(
            flops=2 * count * B * B * HALF, bytes_accessed=4 * MIB * (1 + count), transcendentals=0
        ),
        name="tiles",
    )(info, *rows, *flat, *([extra] if lead else []))


def merge_kernel(info, low, high, after_in, before_in, after, before, held_low, held_high, sems):
    def fill(ref):
        into = [
            pltpu.make_async_copy(low, held_low, sems.at[0]),
            pltpu.make_async_copy(high, held_high, sems.at[1]),
        ]
        out = [
            pltpu.make_async_copy(held_low, ref.at[pl.ds(0, SPLIT)], sems.at[2]),
            pltpu.make_async_copy(held_high, ref.at[pl.ds(SPLIT, B - SPLIT)], sems.at[3]),
        ]
        for copy in into:
            copy.start()
        for k in range(2):
            into[k].wait()
            out[k].start()
        for copy in out:
            copy.wait()

    for side, ref in ((2, after), (1, before)):
        @pl.when(info[0] == side)
        def _(ref=ref):
            fill(ref)


def merge(side, low, high, after, before):
    whole = pl.BlockSpec(memory_space=pl.ANY)
    out = jax.ShapeDtypeStruct((B, WIDE), jnp.bfloat16)
    return pl.pallas_call(
        merge_kernel,
        out_shape=(out, out),
        in_specs=[pl.BlockSpec(memory_space=pltpu.SMEM)] + [whole] * 4,
        out_specs=(whole, whole),
        scratch_shapes=[
            pltpu.VMEM((SPLIT, WIDE), jnp.bfloat16),
            pltpu.VMEM((B - SPLIT, WIDE), jnp.bfloat16),
            pltpu.SemaphoreType.DMA((4,)),
        ],
        input_output_aliases={3: 0, 4: 1},
        compiler_params=pltpu.CompilerParams(vmem_limit_bytes=16 * MIB),
        cost_estimate=pl.CostEstimate(flops=0, bytes_accessed=MIB, transcendentals=0),
        name="merge",
    )(side.astype(jnp.int32).reshape(1), low, high, after, before)


def sum_kernel(slots, near, mid, far, crossed, up, down, far_turned, out_ref):
    pairs = (
        (near[0], crossed[0]),
        (near[1], down[0]),
        (mid[0], up[0]),
        (mid[1], down[1]),
        (mid[2], up[1]),
        (far[0], far_turned[...]),
    )
    for k, (one, two) in enumerate(pairs):
        out_ref[slots[k]] = (one.astype(jnp.float32) + two.astype(jnp.float32)).astype(jnp.bfloat16)


def add_up(slots, *parts):
    whole = pl.BlockSpec(memory_space=pltpu.VMEM)
    return pl.pallas_call(
        sum_kernel,
        out_shape=jax.ShapeDtypeStruct((6, B, B), jnp.bfloat16),
        in_specs=[pl.BlockSpec(memory_space=pltpu.SMEM)] + [whole] * len(parts),
        out_specs=whole,
        compiler_params=pltpu.CompilerParams(vmem_limit_bytes=40 * MIB),
        cost_estimate=pl.CostEstimate(flops=6 * B * B, bytes_accessed=9 * MIB, transcendentals=0),
        name="add_up",
    )(slots, *parts)


def local(features, sources):
    me = lax.axis_index("blk")
    odd = me % 2
    place = (me - SEAM_AT) % SEAM
    spot = me % PLANE
    side = jnp.where(spot < 2, 1, jnp.where(spot >= PLANE - 2, 2, 0))
    own_half = ((me - SEAM_AT) % N) // SEAM
    tags = (sources[:, None] == jnp.arange(TAG, dtype=sources.dtype)[None, :]).astype(jnp.bfloat16)
    keep, other, ahead = make_units(features, tags, own_half, ((me - 2 - SEAM_AT) % N) // SEAM)

    def place_of(i):
        return (i - SEAM_AT) % SEAM

    after2 = send(ahead, lambda i: i - 2, lambda i: corner(i)[1] != 1)
    before2 = send(keep, lambda i: i + 2, lambda i: corner(i)[1] != 2)
    first, second = border_routes(0)
    low = lax.ppermute(lax.slice_in_dim(keep, 0, SPLIT), "blk", first)
    high = lax.ppermute(lax.slice_in_dim(keep, SPLIT, B), "blk", border_routes(1)[0])
    second_half = send(
        keep,
        lambda i: i - PLANE if place_of(i) == 1 else i + SEAM,
        lambda i: place_of(i) < 3,
    )
    opposite = send(hold(other, low, second_half), lambda i: i + SEAM)
    low = lax.ppermute(low, "blk", second)
    second_round = send(second_half, lambda i: i - PLANE, lambda i: place_of(i + PLANE) == 1)
    edge = send(
        hold(keep, low),
        lambda i: i + PLANE if i % 2 else i - PLANE,
        lambda i: i % PLANE in (2, PLANE - 3),
    )
    edge = send(edge, lambda i: i + 3 - PLANE if i % 2 else i - 3 + PLANE, lambda i: i % PLANE in (2, PLANE - 3))
    mate = send(hold(keep, after2, before2, opposite, low, high), lambda i: i ^ 1)

    after2, before2, mate = lax.optimization_barrier((after2, before2, mate))
    after2, before2 = merge(side, low, high, after2, before2)
    before3 = send(before2, lambda i: i + 1, lambda i: i % 2 == 1 and i % PLANE != PLANE - 1)
    after3 = send(after2, lambda i: i - 1, lambda i: i % 2 == 0 and i % PLANE != 0 and place_of(i) != 0)
    after_mate = send(after2, lambda i: i ^ 1)
    before_mate = send(before2, lambda i: i ^ 1)
    lone = send(hold(other, before_mate, after_mate), lambda i: i - 3, lambda i: place_of(i) == 2)

    zero = jnp.zeros((), jnp.int32)
    seam = jnp.where(place == 0, 1, jnp.where(place == 1, 2, 0))
    near, turned0, turned1 = tiles([opposite], [[mate], [after2]], zero, [zero] * 2, ())
    mid, turned2, crossed = tiles(
        [opposite, second_half, second_round],
        [[before2], [after_mate], [before_mate]],
        seam,
        [zero] * 3,
        (0, 2),
        (1, 2),
        turned0,
    )
    far_choice = jnp.where(odd == 1, jnp.where(place == SEAM - 1, 2, 1), 0)
    far_choice = jnp.where((spot == 0) | (spot == PLANE - 1), 3, far_choice)
    far, far_turned = tiles(
        [opposite, second_half],
        [[before3, after3, lone, edge]],
        jnp.where((odd == 0) & (place < 3), 1, 0),
        [far_choice],
        (0,),
    )

    near, mid, far = (send(t, lambda i: i + SEAM) for t in (near, mid, far))
    crossed = send(crossed, lambda i: i ^ 1)
    turned1, turned2, crossed = hold(turned1, before3, after3), hold(turned2, before3, after3), crossed
    up = send(jnp.stack([turned1, crossed[1]]), lambda i: i + 2)
    down = send(jnp.stack([turned2, crossed[2]]), lambda i: i - 2)
    far_turned = send(far_turned, lambda i: i + 3 if i % 2 else i - 3)
    slots = jnp.where(odd == 1, jnp.array([4, 3, 2, 5, 0, 1], jnp.int32), jnp.array([5, 3, 2, 1, 4, 0], jnp.int32))
    return jnp.transpose(add_up(slots, near, mid, far, crossed, up, down, far_turned), (1, 0, 2))


def solution(mesh):
    return jax.shard_map(
        local,
        mesh=mesh,
        in_specs=(P("blk", None), P("blk")),
        out_specs=P("blk", None, None),
        check_vma=False,
    )
```

```python
import jax
import jax.numpy as jnp
from jax import lax
from jax.experimental import pallas as pl
from jax.experimental.pallas import tpu as pltpu
from jax.sharding import PartitionSpec as P

N = 256
SEAM = 128
SEAM_AT = 32
PLANE = 64
B = 512
HALF = 4096
TAG = 128
WIDE = HALF + TAG
NSTEP = 256
ROWS = 64
MIB = 1024 * 1024


def send(block, target, only=None):
    pairs = [(i, target(i) % N) for i in range(N) if only is None or only(i)]
    return lax.ppermute(block, "blk", pairs)


def hold(block, *others):
    return lax.optimization_barrier((block,) + others)[0]


def at(y, z, x, core):
    return ((y % 4 * 8 + z % 8) * 4 + x % 4) * 2 + core


def border_side(i):
    spot = i % PLANE
    return 1 if spot < 2 else 2 if spot >= PLANE - 2 else 0


def border_routes():
    first, second = [], []
    for y in range(4):
        first += [
            (at(y, 0, 0, 1), at(y - 1, 7, 3, 1)),
            (at(y, 7, 3, 1), at(y + 1, 0, 0, 1)),
            (at(y, 0, 0, 0), at(y - 1, 0, 0, 0)),
            (at(y, 7, 3, 0), at(y + 1, 7, 3, 0)),
            (at(y, 7, 2, 1), at(y + 1, 7, 2, 1)),
            (at(y, 0, 1, 0), at(y - 1, 0, 1, 0)),
        ]
        second += [(at(y, 0, 0, 0), at(y, 7, 3, 0)), (at(y, 7, 3, 0), at(y, 0, 0, 0))]
    return first, second


def edge_routes():
    border = [pair for y in range(4) for pair in ((at(y, 7, 2, 1), at(y, 0, 0, 0)), (at(y, 0, 1, 0), at(y, 7, 3, 1)))]
    return border + [(i, (i - 3) % N) for i in range(N) if (i - SEAM_AT) % SEAM == 2]


def unit_kernel(info, x_ref, tag_ref, keep_ref, other_ref, ahead_ref):
    x = x_ref[...].astype(jnp.float32)
    squares = jnp.sum(x * x, axis=1, keepdims=True)
    unit = (x * (1.0 / jnp.sqrt(squares + 1e-06))).astype(jnp.bfloat16)
    low, high = unit[:, :HALF], unit[:, HALF:]
    tag = tag_ref[...]

    def put(ref, half):
        @pl.when(half == 0)
        def _():
            ref[:, :HALF] = low

        @pl.when(half != 0)
        def _():
            ref[:, :HALF] = high

        ref[:, HALF:] = tag

    put(keep_ref, info[0])
    put(other_ref, 1 - info[0])
    put(ahead_ref, info[1])


def make_units(features, tags, own_half, ahead_half):
    out = jax.ShapeDtypeStruct((B, WIDE), jnp.bfloat16)
    spec = pl.BlockSpec((ROWS, WIDE), lambda r, info: (r, 0))
    return pl.pallas_call(
        unit_kernel,
        out_shape=(out, out, out),
        grid_spec=pltpu.PrefetchScalarGridSpec(
            num_scalar_prefetch=1,
            grid=(B // ROWS,),
            in_specs=[
                pl.BlockSpec((ROWS, 2 * HALF), lambda r, info: (r, 0)),
                pl.BlockSpec((ROWS, TAG), lambda r, info: (r, 0)),
            ],
            out_specs=(spec, spec, spec),
        ),
        compiler_params=pltpu.CompilerParams(vmem_limit_bytes=40 * MIB),
        cost_estimate=pl.CostEstimate(flops=12 * B * HALF, bytes_accessed=20 * MIB, transcendentals=B),
        name="units",
    )(jnp.stack([own_half, ahead_half]).astype(jnp.int32), features, tags)


def tiles(rows, blocks, row_choice, block_choice, seam_tiles, stacked=()):
    count = len(blocks)
    used_rows = len(rows)
    blocks = [[option if isinstance(option, tuple) else (option,) for option in entry] for entry in blocks]
    flat = [array for entry in blocks for option in entry for array in option]
    alone = [t for t in range(count) if t not in stacked]

    def kernel(info, *refs):
        row_refs = refs[:used_rows]
        block_refs = []
        at_ref = used_rows
        for entry in blocks:
            block_refs.append([])
            for option in entry:
                block_refs[-1].append(refs[at_ref : at_ref + len(option)])
                at_ref += len(option)
        out_ref = refs[at_ref]
        turned = {t: refs[at_ref + 1 + k] for k, t in enumerate(alone)}
        at_ref += 1 + len(alone)
        if stacked:
            for k, t in enumerate(stacked):
                turned[t] = refs[at_ref].at[k]
            at_ref += 1
        held_rows, held_blocks, row_sems, block_sems = refs[at_ref:]

        pltpu.make_async_copy(row_refs[0], held_rows.at[0], row_sems.at[0]).start()
        for t in range(count):
            for c, pieces in enumerate(block_refs[t]):
                @pl.when(info[1 + t] == c)
                def _(t=t, pieces=pieces):
                    row = 0
                    for ref in pieces:
                        into = held_blocks.at[t, pl.ds(row, ref.shape[0])]
                        pltpu.make_async_copy(ref, into, block_sems.at[t]).start()
                        row += ref.shape[0]
            if t == 0:
                for c in range(1, used_rows):
                    @pl.when(info[0] == c)
                    def _(c=c):
                        pltpu.make_async_copy(row_refs[c], held_rows.at[1], row_sems.at[1]).start()

        pltpu.make_async_copy(row_refs[0], held_rows.at[0], row_sems.at[0]).wait()
        waited = False
        for t in range(count):
            which = 0
            if t in seam_tiles:
                if not waited:
                    @pl.when(info[0] > 0)
                    def _():
                        pltpu.make_async_copy(row_refs[0], held_rows.at[1], row_sems.at[1]).wait()
                    waited = True
                which = jnp.minimum(info[0], 1)
            pltpu.make_async_copy(held_blocks.at[t], held_blocks.at[t], block_sems.at[t]).wait()

            def chunk(n, _, t=t, which=which):
                span = pl.ds(pl.multiple_of(n * NSTEP, NSTEP), NSTEP)
                over = (((1,), (1,)), ((), ()))
                tile = lax.dot_general(
                    held_rows[which, :, :HALF], held_blocks[t, span, :HALF], over, preferred_element_type=jnp.float32
                )
                same = lax.dot_general(
                    held_rows[which, :, HALF:], held_blocks[t, span, HALF:], over, preferred_element_type=jnp.float32
                )
                tile = jnp.where(same > 0.5, jnp.float32(0.0), tile)
                out_ref[t, :, span] = tile.astype(jnp.bfloat16)
                turned[t][span, :] = tile.T.astype(jnp.bfloat16)
                return 0

            lax.fori_loop(0, B // NSTEP, chunk, 0)

    one = jax.ShapeDtypeStruct((B, B), jnp.bfloat16)
    whole = pl.BlockSpec(memory_space=pltpu.VMEM)
    info = jnp.stack([row_choice] + list(block_choice)).astype(jnp.int32)
    outs = (jax.ShapeDtypeStruct((count, B, B), jnp.bfloat16),) + (one,) * len(alone)
    if stacked:
        outs += (jax.ShapeDtypeStruct((len(stacked), B, B), jnp.bfloat16),)
    return pl.pallas_call(
        kernel,
        out_shape=outs,
        in_specs=[pl.BlockSpec(memory_space=pltpu.SMEM)]
        + [pl.BlockSpec(memory_space=pl.ANY)] * (used_rows + len(flat)),
        out_specs=(whole,) * len(outs),
        scratch_shapes=[
            pltpu.VMEM((2, B, WIDE), jnp.bfloat16),
            pltpu.VMEM((count, B, WIDE), jnp.bfloat16),
            pltpu.SemaphoreType.DMA((2,)),
            pltpu.SemaphoreType.DMA((count,)),
        ],
        compiler_params=pltpu.CompilerParams(vmem_limit_bytes=50 * MIB),
        cost_estimate=pl.CostEstimate(
            flops=2 * count * B * B * HALF, bytes_accessed=4 * MIB * (1 + count), transcendentals=0
        ),
        name="tiles",
    )(info, *rows, *flat)


def merge_kernel(info, even, odd, after_in, before_in, after, before, held, sems):
    for side, ref in ((2, after), (1, before)):
        for core, source in ((0, even), (1, odd)):
            @pl.when((info[0] == side) & (info[1] == core))
            def _(ref=ref, source=source):
                for out in (False, True):
                    copies = []
                    for k in range(4):
                        rows = pl.ds(k * B // 4, B // 4)
                        pair = (held.at[rows], ref.at[rows]) if out else (source.at[rows], held.at[rows])
                        copies.append(pltpu.make_async_copy(*pair, sems.at[k]))
                    for copy in copies:
                        copy.start()
                    for copy in copies:
                        copy.wait()


def merge(side, core, even, odd, after, before):
    whole = pl.BlockSpec(memory_space=pl.ANY)
    out = jax.ShapeDtypeStruct((B, WIDE), jnp.bfloat16)
    return pl.pallas_call(
        merge_kernel,
        out_shape=(out, out),
        in_specs=[pl.BlockSpec(memory_space=pltpu.SMEM)] + [whole] * 4,
        out_specs=(whole, whole),
        scratch_shapes=[pltpu.VMEM((B, WIDE), jnp.bfloat16), pltpu.SemaphoreType.DMA((4,))],
        input_output_aliases={3: 0, 4: 1},
        compiler_params=pltpu.CompilerParams(vmem_limit_bytes=16 * MIB),
        cost_estimate=pl.CostEstimate(flops=0, bytes_accessed=MIB, transcendentals=0),
        name="merge",
    )(jnp.stack([side, core]).astype(jnp.int32), even, odd, after, before)


def sum_kernel(slots, near, far, crossed, up, down, far_turned, out_ref):
    pairs = (
        (near[2], crossed[0]),
        (near[0], down[0]),
        (near[1], up[0]),
        (near[3], down[1]),
        (near[4], up[1]),
        (far[0], far_turned[...]),
    )
    for k, (one, two) in enumerate(pairs):
        out_ref[slots[k]] = (one.astype(jnp.float32) + two.astype(jnp.float32)).astype(jnp.bfloat16)


def add_up(slots, *parts):
    whole = pl.BlockSpec(memory_space=pltpu.VMEM)
    return pl.pallas_call(
        sum_kernel,
        out_shape=jax.ShapeDtypeStruct((6, B, B), jnp.bfloat16),
        in_specs=[pl.BlockSpec(memory_space=pltpu.SMEM)] + [whole] * len(parts),
        out_specs=whole,
        compiler_params=pltpu.CompilerParams(vmem_limit_bytes=40 * MIB),
        cost_estimate=pl.CostEstimate(flops=6 * B * B, bytes_accessed=9 * MIB, transcendentals=0),
        name="add_up",
    )(slots, *parts)


def local(features, sources):
    me = lax.axis_index("blk")
    odd = me % 2
    place = (me - SEAM_AT) % SEAM
    spot = me % PLANE
    side = jnp.where(spot < 2, 1, jnp.where(spot >= PLANE - 2, 2, 0))
    own_half = ((me - SEAM_AT) % N) // SEAM
    tags = (sources[:, None] == jnp.arange(TAG, dtype=sources.dtype)[None, :]).astype(jnp.bfloat16)
    keep, other, ahead = make_units(features, tags, own_half, ((me - 2 - SEAM_AT) % N) // SEAM)

    def place_of(i):
        return (i - SEAM_AT) % SEAM

    after2 = send(ahead, lambda i: i - 2, lambda i: border_side(i) != 1)
    before2 = send(keep, lambda i: i + 2, lambda i: border_side(i) != 2)
    first, second = border_routes()
    crossed_once = lax.ppermute(keep, "blk", first)
    second_half = send(
        keep,
        lambda i: i - PLANE if place_of(i) == 1 else i + SEAM,
        lambda i: place_of(i) < 3,
    )
    opposite = send(hold(other, crossed_once), lambda i: i + SEAM)
    crossed_twice = lax.ppermute(crossed_once, "blk", second)
    edge = lax.ppermute(jnp.where(place == 2, other, crossed_once), "blk", edge_routes())
    mate = send(hold(keep, after2, before2, opposite, second_half, crossed_twice), lambda i: i ^ 1)
    after2, before2, mate = lax.optimization_barrier((after2, before2, mate))
    after2, before2 = merge(side, odd, crossed_twice, crossed_once, after2, before2)
    before3 = send(before2, lambda i: i + 1, lambda i: i % 2 == 1 and i % PLANE != PLANE - 1)
    after3 = send(after2, lambda i: i - 1, lambda i: i % 2 == 0 and i % PLANE != 0 and place_of(i) != 0)
    after_mate = send(after2, lambda i: i ^ 1)
    before_mate = send(before2, lambda i: i ^ 1)
    second_round = send(hold(second_half, mate), lambda i: i - PLANE, lambda i: place_of(i + PLANE) == 1)

    zero = jnp.zeros((), jnp.int32)
    seam = jnp.where(place == 0, 1, jnp.where(place == 1, 2, 0))
    near, turned1, turned2, crossed = tiles(
        [opposite, second_half, second_round],
        [[after2], [before2], [mate], [after_mate], [before_mate]],
        seam,
        [zero] * 5,
        (1, 4),
        (2, 3, 4),
    )
    far_choice = jnp.where((spot == 0) | (spot == PLANE - 1) | (place == SEAM - 1), 2, odd)
    far, far_turned = tiles(
        [hold(opposite, near), second_half],
        [[before3, after3, edge]],
        jnp.where((odd == 0) & (place < 3), 1, 0),
        [far_choice],
        (0,),
    )

    near = send(near, lambda i: i + SEAM)
    far = send(far, lambda i: i + SEAM)
    crossed = send(crossed, lambda i: i ^ 1)
    turned1, turned2, crossed = hold(turned1, before3, after3), hold(turned2, before3, after3), crossed
    up = send(jnp.stack([turned1, crossed[1]]), lambda i: i + 2)
    down = send(jnp.stack([turned2, crossed[2]]), lambda i: i - 2)
    far_turned = send(far_turned, lambda i: i + 3 if i % 2 else i - 3)
    slots = jnp.where(odd == 1, jnp.array([4, 3, 2, 5, 0, 1], jnp.int32), jnp.array([5, 3, 2, 1, 4, 0], jnp.int32))
    return jnp.transpose(add_up(slots, near, far, crossed, up, down, far_turned), (1, 0, 2))


def solution(mesh):
    return jax.shard_map(
        local,
        mesh=mesh,
        in_specs=(P("blk", None), P("blk")),
        out_specs=P("blk", None, None),
        check_vma=False,
    )
```

```python
import jax
import jax.numpy as jnp
from jax import lax
from jax.experimental import pallas as pl
from jax.experimental.pallas import tpu as pltpu
from jax.sharding import PartitionSpec as P

N = 256
SEAM = 128
SEAM_AT = 32
PLANE = 64
B = 512
HALF = 4096
TAG = 128
WIDE = HALF + TAG
NSTEP = 256
ROWS = 64
MIB = 1024 * 1024


def send(block, target, only=None):
    pairs = [(i, target(i) % N) for i in range(N) if only is None or only(i)]
    return lax.ppermute(block, "blk", pairs)


def hold(block, *others):
    return lax.optimization_barrier((block,) + others)[0]


def at(y, z, x, core):
    return ((y % 4 * 8 + z % 8) * 4 + x % 4) * 2 + core


def border_side(i):
    spot = i % PLANE
    return 1 if spot < 2 else 2 if spot >= PLANE - 2 else 0


def border_routes():
    first, second = [], []
    for y in range(4):
        first += [
            (at(y, 0, 0, 1), at(y - 1, 7, 3, 1)),
            (at(y, 7, 3, 1), at(y + 1, 0, 0, 1)),
            (at(y, 0, 0, 0), at(y - 1, 0, 0, 0)),
            (at(y, 7, 3, 0), at(y + 1, 7, 3, 0)),
            (at(y, 7, 2, 1), at(y + 1, 7, 2, 1)),
            (at(y, 0, 1, 0), at(y - 1, 0, 1, 0)),
        ]
        second += [(at(y, 0, 0, 0), at(y, 7, 3, 0)), (at(y, 7, 3, 0), at(y, 0, 0, 0))]
    return first, second


def edge_routes():
    border = [pair for y in range(4) for pair in ((at(y, 7, 2, 1), at(y, 0, 0, 0)), (at(y, 0, 1, 0), at(y, 7, 3, 1)))]
    return border + [(i, (i - 3) % N) for i in range(N) if (i - SEAM_AT) % SEAM == 2]


def unit_kernel(info, x_ref, tag_ref, keep_ref, other_ref, ahead_ref):
    x = x_ref[...].astype(jnp.float32)
    squares = jnp.sum(x * x, axis=1, keepdims=True)
    unit = (x * (1.0 / jnp.sqrt(squares + 1e-06))).astype(jnp.bfloat16)
    low, high = unit[:, :HALF], unit[:, HALF:]
    tag = tag_ref[...]

    def put(ref, half):
        @pl.when(half == 0)
        def _():
            ref[:, :HALF] = low

        @pl.when(half != 0)
        def _():
            ref[:, :HALF] = high

        ref[:, HALF:] = tag

    put(keep_ref, info[0])
    put(other_ref, 1 - info[0])
    put(ahead_ref, info[1])


def make_units(features, tags, own_half, ahead_half):
    out = jax.ShapeDtypeStruct((B, WIDE), jnp.bfloat16)
    spec = pl.BlockSpec((ROWS, WIDE), lambda r, info: (r, 0))
    return pl.pallas_call(
        unit_kernel,
        out_shape=(out, out, out),
        grid_spec=pltpu.PrefetchScalarGridSpec(
            num_scalar_prefetch=1,
            grid=(B // ROWS,),
            in_specs=[
                pl.BlockSpec((ROWS, 2 * HALF), lambda r, info: (r, 0)),
                pl.BlockSpec((ROWS, TAG), lambda r, info: (r, 0)),
            ],
            out_specs=(spec, spec, spec),
        ),
        compiler_params=pltpu.CompilerParams(vmem_limit_bytes=40 * MIB),
        cost_estimate=pl.CostEstimate(flops=12 * B * HALF, bytes_accessed=20 * MIB, transcendentals=B),
        name="units",
    )(jnp.stack([own_half, ahead_half]).astype(jnp.int32), features, tags)


def tiles(rows, blocks, row_choice, block_choice, seam_tiles, stacked=(), short=False):
    count = len(blocks)
    used_rows = len(rows)
    blocks = [[option if isinstance(option, tuple) else (option,) for option in entry] for entry in blocks]
    flat = [array for entry in blocks for option in entry for array in option]
    alone = [t for t in range(count) if t not in stacked]

    def kernel(info, *refs):
        row_refs = refs[:used_rows]
        block_refs = []
        at_ref = used_rows
        for entry in blocks:
            block_refs.append([])
            for option in entry:
                block_refs[-1].append(refs[at_ref : at_ref + len(option)])
                at_ref += len(option)
        out_ref = refs[at_ref]
        turned = {t: refs[at_ref + 1 + k] for k, t in enumerate(alone)}
        at_ref += 1 + len(alone)
        if stacked:
            for k, t in enumerate(stacked):
                turned[t] = refs[at_ref].at[k]
            at_ref += 1
        held_rows, held_blocks, row_sems, block_sems = refs[at_ref:]

        pltpu.make_async_copy(row_refs[0], held_rows.at[0], row_sems.at[0]).start()
        for t in range(count):
            for c, pieces in enumerate(block_refs[t]):
                @pl.when(info[1 + t] == c)
                def _(t=t, pieces=pieces):
                    row = 0
                    for ref in pieces:
                        into = held_blocks.at[t, pl.ds(row, ref.shape[0])]
                        pltpu.make_async_copy(ref, into, block_sems.at[t]).start()
                        row += ref.shape[0]
            if t == 0:
                for c in range(1, used_rows):
                    @pl.when(info[0] == c)
                    def _(c=c):
                        pltpu.make_async_copy(row_refs[c], held_rows.at[1], row_sems.at[1]).start()

        pltpu.make_async_copy(row_refs[0], held_rows.at[0], row_sems.at[0]).wait()
        waited = False
        for t in range(count):
            which = 0
            if t in seam_tiles:
                if not waited:
                    @pl.when(info[0] > 0)
                    def _():
                        pltpu.make_async_copy(row_refs[0], held_rows.at[1], row_sems.at[1]).wait()
                    waited = True
                which = jnp.minimum(info[0], 1)
            pltpu.make_async_copy(held_blocks.at[t], held_blocks.at[t], block_sems.at[t]).wait()

            def chunk(n, _, t=t, which=which):
                span = pl.ds(pl.multiple_of(n * NSTEP, NSTEP), NSTEP)
                over = (((1,), (1,)), ((), ()))
                tile = lax.dot_general(
                    held_rows[which, :, :HALF], held_blocks[t, span, :HALF], over, preferred_element_type=jnp.float32
                )
                same = lax.dot_general(
                    held_rows[which, :, HALF:], held_blocks[t, span, HALF:], over, preferred_element_type=jnp.float32
                )
                tile = jnp.where(same > 0.5, jnp.float32(0.0), tile)
                out_ref[t, :, span] = tile.astype(jnp.bfloat16)
                turned[t][span, :] = tile.T.astype(jnp.bfloat16)
                return 0

            lax.fori_loop(0, B // NSTEP, chunk, 0)

    one = jax.ShapeDtypeStruct((B, B), jnp.bfloat16)
    whole = pl.BlockSpec(memory_space=pltpu.VMEM)
    info = jnp.stack([row_choice] + list(block_choice)).astype(jnp.int32)
    outs = (jax.ShapeDtypeStruct((count, B, B), jnp.bfloat16),) + (one,) * len(alone)
    if stacked:
        outs += (jax.ShapeDtypeStruct((len(stacked), B, B), jnp.bfloat16),)
    return pl.pallas_call(
        kernel,
        out_shape=outs,
        in_specs=[pl.BlockSpec(memory_space=pltpu.SMEM)]
        + [pl.BlockSpec(memory_space=pl.ANY)] * (used_rows + len(flat)),
        out_specs=(whole,) * len(outs),
        scratch_shapes=[
            pltpu.VMEM((2, B, WIDE), jnp.bfloat16),
            pltpu.VMEM((count, B, WIDE), jnp.bfloat16),
            pltpu.SemaphoreType.DMA((2,)),
            pltpu.SemaphoreType.DMA((count,)),
        ],
        compiler_params=pltpu.CompilerParams(vmem_limit_bytes=50 * MIB),
        cost_estimate=pl.CostEstimate(
            flops=0 if short else 2 * count * B * B * HALF,
            bytes_accessed=MIB if short else 4 * MIB * (1 + count),
            transcendentals=0,
        ),
        name="tiles",
    )(info, *rows, *flat)


def merge_kernel(info, even, odd, after_in, before_in, after, before, held, sems):
    for side, ref in ((2, after), (1, before)):
        for core, source in ((0, even), (1, odd)):
            @pl.when((info[0] == side) & (info[1] == core))
            def _(ref=ref, source=source):
                into, out = [], []
                for k in range(8):
                    rows = pl.ds(k * B // 8, B // 8)
                    into.append(pltpu.make_async_copy(source.at[rows], held.at[rows], sems.at[k]))
                    out.append(pltpu.make_async_copy(held.at[rows], ref.at[rows], sems.at[8 + k]))
                for copy in into:
                    copy.start()
                for k in range(8):
                    into[k].wait()
                    out[k].start()
                for copy in out:
                    copy.wait()


def merge(side, core, even, odd, after, before):
    whole = pl.BlockSpec(memory_space=pl.ANY)
    out = jax.ShapeDtypeStruct((B, WIDE), jnp.bfloat16)
    return pl.pallas_call(
        merge_kernel,
        out_shape=(out, out),
        in_specs=[pl.BlockSpec(memory_space=pltpu.SMEM)] + [whole] * 4,
        out_specs=(whole, whole),
        scratch_shapes=[pltpu.VMEM((B, WIDE), jnp.bfloat16), pltpu.SemaphoreType.DMA((16,))],
        input_output_aliases={3: 0, 4: 1},
        compiler_params=pltpu.CompilerParams(vmem_limit_bytes=16 * MIB),
        cost_estimate=pl.CostEstimate(flops=0, bytes_accessed=MIB, transcendentals=0),
        name="merge",
    )(jnp.stack([side, core]).astype(jnp.int32), even, odd, after, before)


def sum_kernel(slots, near, mid, far, crossed, up, down, far_turned, out_ref):
    pairs = (
        (near[0], crossed[0]),
        (near[1], down[0]),
        (mid[0], up[0]),
        (mid[1], down[1]),
        (mid[2], up[1]),
        (far[0], far_turned[...]),
    )
    for k, (one, two) in enumerate(pairs):
        out_ref[slots[k]] = (one.astype(jnp.float32) + two.astype(jnp.float32)).astype(jnp.bfloat16)


def add_up(slots, *parts):
    whole = pl.BlockSpec(memory_space=pltpu.VMEM)
    return pl.pallas_call(
        sum_kernel,
        out_shape=jax.ShapeDtypeStruct((6, B, B), jnp.bfloat16),
        in_specs=[pl.BlockSpec(memory_space=pltpu.SMEM)] + [whole] * len(parts),
        out_specs=whole,
        compiler_params=pltpu.CompilerParams(vmem_limit_bytes=40 * MIB),
        cost_estimate=pl.CostEstimate(flops=6 * B * B, bytes_accessed=9 * MIB, transcendentals=0),
        name="add_up",
    )(slots, *parts)


def local(features, sources):
    me = lax.axis_index("blk")
    odd = me % 2
    place = (me - SEAM_AT) % SEAM
    spot = me % PLANE
    side = jnp.where(spot < 2, 1, jnp.where(spot >= PLANE - 2, 2, 0))
    own_half = ((me - SEAM_AT) % N) // SEAM
    tags = (sources[:, None] == jnp.arange(TAG, dtype=sources.dtype)[None, :]).astype(jnp.bfloat16)
    keep, other, ahead = make_units(features, tags, own_half, ((me - 2 - SEAM_AT) % N) // SEAM)

    def place_of(i):
        return (i - SEAM_AT) % SEAM

    after2 = send(ahead, lambda i: i - 2, lambda i: border_side(i) != 1)
    before2 = send(keep, lambda i: i + 2, lambda i: border_side(i) != 2)
    first, second = border_routes()
    crossed_once = lax.ppermute(keep, "blk", first)
    second_half = send(
        keep,
        lambda i: i - PLANE if place_of(i) == 1 else i + SEAM,
        lambda i: place_of(i) < 3,
    )
    opposite = send(hold(other, crossed_once), lambda i: i + SEAM)
    crossed_twice = lax.ppermute(crossed_once, "blk", second)
    mate = send(hold(keep, after2, before2, opposite, second_half, crossed_twice), lambda i: i ^ 1)
    second_round = send(
        hold(second_half, after2, before2, opposite), lambda i: i - PLANE, lambda i: place_of(i + PLANE) == 1
    )
    edge = jnp.where(place == 2, other, crossed_once)
    after2, before2, mate, edge = lax.optimization_barrier((after2, before2, mate, edge))
    after2, before2 = merge(side, odd, crossed_twice, crossed_once, after2, before2)
    before3 = send(before2, lambda i: i + 1, lambda i: i % 2 == 1 and i % PLANE != PLANE - 1)
    after3 = send(after2, lambda i: i - 1, lambda i: i % 2 == 0 and i % PLANE != 0 and place_of(i) != 0)
    after_mate = send(after2, lambda i: i ^ 1)
    before_mate = send(before2, lambda i: i ^ 1)

    zero = jnp.zeros((), jnp.int32)
    seam = jnp.where(place == 0, 1, jnp.where(place == 1, 2, 0))
    rows = [opposite, second_half, second_round]
    rows = [opposite, second_half, second_round]
    near, turned0, turned1 = tiles(rows[:1], [[mate], [after2]], zero, [zero] * 2, ())
    edge = lax.ppermute(hold(edge, turned1), "blk", edge_routes())
    mid, turned2, crossed = tiles(
        [hold(opposite, near)] + rows[1:],
        [[before2], [after_mate], [before_mate]],
        seam,
        [zero] * 3,
        (0, 2),
        (1, 2),
        True,
    )
    crossed = jnp.concatenate([turned0[None], crossed])
    far_choice = jnp.where((spot == 0) | (spot == PLANE - 1) | (place == SEAM - 1), 2, odd)
    far, far_turned = tiles(
        [hold(opposite, mid), second_half],
        [[before3, after3, edge]],
        jnp.where((odd == 0) & (place < 3), 1, 0),
        [far_choice],
        (0,),
    )

    near = send(near, lambda i: i + SEAM)
    mid = send(mid, lambda i: i + SEAM)
    crossed = hold(crossed, near)
    far = send(far, lambda i: i + SEAM)
    crossed = send(crossed, lambda i: i ^ 1)
    turned1, turned2, crossed = hold(turned1, before3, after3), hold(turned2, before3, after3), crossed
    up = send(jnp.stack([turned1, crossed[1]]), lambda i: i + 2)
    down = send(jnp.stack([turned2, crossed[2]]), lambda i: i - 2)
    far_turned = send(far_turned, lambda i: i + 3 if i % 2 else i - 3)
    slots = jnp.where(odd == 1, jnp.array([4, 3, 2, 5, 0, 1], jnp.int32), jnp.array([5, 3, 2, 1, 4, 0], jnp.int32))
    return jnp.transpose(add_up(slots, near, mid, far, crossed, up, down, far_turned), (1, 0, 2))


def solution(mesh):
    return jax.shard_map(
        local,
        mesh=mesh,
        in_specs=(P("blk", None), P("blk")),
        out_specs=P("blk", None, None),
        check_vma=False,
    )
```

```python
import jax
import jax.numpy as jnp
from jax import lax
from jax.experimental import pallas as pl
from jax.experimental.pallas import tpu as pltpu
from jax.sharding import PartitionSpec as P

N = 256
SEAM = 128
SEAM_AT = 32
PLANE = 64
B = 512
HALF = 4096
TAG = 128
WIDE = HALF + TAG
NSTEP = 256
ROWS = 64
PIECE = 512
MIB = 1024 * 1024


def send(block, target, only=None):
    pairs = [(i, target(i) % N) for i in range(N) if only is None or only(i)]
    return lax.ppermute(block, "blk", pairs)


def hold(block, *others):
    return lax.optimization_barrier((block,) + others)[0]


def at(y, z, x, core):
    return ((y % 4 * 8 + z % 8) * 4 + x % 4) * 2 + core


def border_side(i):
    spot = i % PLANE
    return 1 if spot < 2 else 2 if spot >= PLANE - 2 else 0


def border_routes():
    first, second = [], []
    for y in range(4):
        first += [
            (at(y, 0, 0, 1), at(y - 1, 7, 3, 1)),
            (at(y, 7, 3, 1), at(y + 1, 0, 0, 1)),
            (at(y, 0, 0, 0), at(y - 1, 0, 0, 0)),
            (at(y, 7, 3, 0), at(y + 1, 7, 3, 0)),
            (at(y, 7, 2, 1), at(y + 1, 7, 2, 1)),
            (at(y, 0, 1, 0), at(y - 1, 0, 1, 0)),
        ]
        second += [(at(y, 0, 0, 0), at(y, 7, 3, 0)), (at(y, 7, 3, 0), at(y, 0, 0, 0))]
    return first, second


def edge_routes():
    border = [pair for y in range(4) for pair in ((at(y, 7, 2, 1), at(y, 0, 0, 0)), (at(y, 0, 1, 0), at(y, 7, 3, 1)))]
    return border + [(i, (i - 3) % N) for i in range(N) if (i - SEAM_AT) % SEAM == 2]


def unit_kernel(info, x_ref, tag_ref, keep_ref, other_ref, ahead_ref):
    same = info[0] == info[1]
    starts = [pl.multiple_of(half * HALF, HALF) for half in (info[0], 1 - info[0])]

    def some_rows(r, _):
        span = pl.ds(pl.multiple_of(r * 16, 16), 16)
        total = jnp.zeros((16, PIECE), jnp.float32)
        for c in range(2 * HALF // PIECE):
            x = x_ref[span, c * PIECE : (c + 1) * PIECE].astype(jnp.float32)
            total += x * x
        scale = 1.0 / jnp.sqrt(jnp.sum(total, axis=1, keepdims=True) + 1e-06)
        for c in range(HALF // PIECE):
            put = slice(c * PIECE, (c + 1) * PIECE)
            own, rest = (
                x_ref[span, pl.ds(start + c * PIECE, PIECE)].astype(jnp.float32) * scale for start in starts
            )
            keep_ref[span, put] = own.astype(jnp.bfloat16)
            other_ref[span, put] = rest.astype(jnp.bfloat16)
            ahead_ref[span, put] = jnp.where(same, own, rest).astype(jnp.bfloat16)
        for ref in (keep_ref, other_ref, ahead_ref):
            ref[span, HALF:] = tag_ref[span, :]
        return 0

    lax.fori_loop(0, ROWS // 16, some_rows, 0)


def make_units(features, tags, own_half, ahead_half):
    out = jax.ShapeDtypeStruct((B, WIDE), jnp.bfloat16)
    spec = pl.BlockSpec((ROWS, WIDE), lambda r, info: (r, 0))
    return pl.pallas_call(
        unit_kernel,
        out_shape=(out, out, out),
        grid_spec=pltpu.PrefetchScalarGridSpec(
            num_scalar_prefetch=1,
            grid=(B // ROWS,),
            in_specs=[
                pl.BlockSpec((ROWS, 2 * HALF), lambda r, info: (r, 0)),
                pl.BlockSpec((ROWS, TAG), lambda r, info: (r, 0)),
            ],
            out_specs=(spec, spec, spec),
        ),
        compiler_params=pltpu.CompilerParams(vmem_limit_bytes=40 * MIB),
        cost_estimate=pl.CostEstimate(flops=12 * B * HALF, bytes_accessed=20 * MIB, transcendentals=B),
        name="units",
    )(jnp.stack([own_half, ahead_half]).astype(jnp.int32), features, tags)


def tiles(rows, blocks, row_choice, block_choice, seam_tiles, stacked=(), short=False):
    count = len(blocks)
    used_rows = len(rows)
    blocks = [[option if isinstance(option, tuple) else (option,) for option in entry] for entry in blocks]
    flat = [array for entry in blocks for option in entry for array in option]
    alone = [t for t in range(count) if t not in stacked]

    def kernel(info, *refs):
        row_refs = refs[:used_rows]
        block_refs = []
        at_ref = used_rows
        for entry in blocks:
            block_refs.append([])
            for option in entry:
                block_refs[-1].append(refs[at_ref : at_ref + len(option)])
                at_ref += len(option)
        out_ref = refs[at_ref]
        turned = {t: refs[at_ref + 1 + k] for k, t in enumerate(alone)}
        at_ref += 1 + len(alone)
        if stacked:
            for k, t in enumerate(stacked):
                turned[t] = refs[at_ref].at[k]
            at_ref += 1
        held_rows, held_blocks, row_sems, block_sems = refs[at_ref:]

        pltpu.make_async_copy(row_refs[0], held_rows.at[0], row_sems.at[0]).start()
        for t in range(count):
            for c, pieces in enumerate(block_refs[t]):
                @pl.when(info[1 + t] == c)
                def _(t=t, pieces=pieces):
                    row = 0
                    for ref in pieces:
                        into = held_blocks.at[t, pl.ds(row, ref.shape[0])]
                        pltpu.make_async_copy(ref, into, block_sems.at[t]).start()
                        row += ref.shape[0]
            if t == 0:
                for c in range(1, used_rows):
                    @pl.when(info[0] == c)
                    def _(c=c):
                        pltpu.make_async_copy(row_refs[c], held_rows.at[1], row_sems.at[1]).start()

        pltpu.make_async_copy(row_refs[0], held_rows.at[0], row_sems.at[0]).wait()
        waited = False
        for t in range(count):
            which = 0
            if t in seam_tiles:
                if not waited:
                    @pl.when(info[0] > 0)
                    def _():
                        pltpu.make_async_copy(row_refs[0], held_rows.at[1], row_sems.at[1]).wait()
                    waited = True
                which = jnp.minimum(info[0], 1)
            pltpu.make_async_copy(held_blocks.at[t], held_blocks.at[t], block_sems.at[t]).wait()

            def chunk(n, _, t=t, which=which):
                span = pl.ds(pl.multiple_of(n * NSTEP, NSTEP), NSTEP)
                over = (((1,), (1,)), ((), ()))
                tile = lax.dot_general(
                    held_rows[which, :, :HALF], held_blocks[t, span, :HALF], over, preferred_element_type=jnp.float32
                )
                same = lax.dot_general(
                    held_rows[which, :, HALF:], held_blocks[t, span, HALF:], over, preferred_element_type=jnp.float32
                )
                tile = jnp.where(same > 0.5, jnp.float32(0.0), tile)
                out_ref[t, :, span] = tile.astype(jnp.bfloat16)
                turned[t][span, :] = tile.T.astype(jnp.bfloat16)
                return 0

            lax.fori_loop(0, B // NSTEP, chunk, 0)

    one = jax.ShapeDtypeStruct((B, B), jnp.bfloat16)
    whole = pl.BlockSpec(memory_space=pltpu.VMEM)
    info = jnp.stack([row_choice] + list(block_choice)).astype(jnp.int32)
    outs = (jax.ShapeDtypeStruct((count, B, B), jnp.bfloat16),) + (one,) * len(alone)
    if stacked:
        outs += (jax.ShapeDtypeStruct((len(stacked), B, B), jnp.bfloat16),)
    return pl.pallas_call(
        kernel,
        out_shape=outs,
        in_specs=[pl.BlockSpec(memory_space=pltpu.SMEM)]
        + [pl.BlockSpec(memory_space=pl.ANY)] * (used_rows + len(flat)),
        out_specs=(whole,) * len(outs),
        scratch_shapes=[
            pltpu.VMEM((2, B, WIDE), jnp.bfloat16),
            pltpu.VMEM((count, B, WIDE), jnp.bfloat16),
            pltpu.SemaphoreType.DMA((2,)),
            pltpu.SemaphoreType.DMA((count,)),
        ],
        compiler_params=pltpu.CompilerParams(vmem_limit_bytes=50 * MIB),
        cost_estimate=pl.CostEstimate(
            flops=0 if short else 2 * count * B * B * HALF,
            bytes_accessed=MIB if short else 4 * MIB * (1 + count),
            transcendentals=0,
        ),
        name="tiles",
    )(info, *rows, *flat)


def merge_kernel(info, even, odd, after_in, before_in, after, before, held, sems):
    for side, ref in ((2, after), (1, before)):
        for core, source in ((0, even), (1, odd)):
            @pl.when((info[0] == side) & (info[1] == core))
            def _(ref=ref, source=source):
                into, out = [], []
                for k in range(8):
                    rows = pl.ds(k * B // 8, B // 8)
                    into.append(pltpu.make_async_copy(source.at[rows], held.at[rows], sems.at[k]))
                    out.append(pltpu.make_async_copy(held.at[rows], ref.at[rows], sems.at[8 + k]))
                for copy in into:
                    copy.start()
                for k in range(8):
                    into[k].wait()
                    out[k].start()
                for copy in out:
                    copy.wait()


def merge(side, core, even, odd, after, before):
    whole = pl.BlockSpec(memory_space=pl.ANY)
    out = jax.ShapeDtypeStruct((B, WIDE), jnp.bfloat16)
    return pl.pallas_call(
        merge_kernel,
        out_shape=(out, out),
        in_specs=[pl.BlockSpec(memory_space=pltpu.SMEM)] + [whole] * 4,
        out_specs=(whole, whole),
        scratch_shapes=[pltpu.VMEM((B, WIDE), jnp.bfloat16), pltpu.SemaphoreType.DMA((16,))],
        input_output_aliases={3: 0, 4: 1},
        compiler_params=pltpu.CompilerParams(vmem_limit_bytes=16 * MIB),
        cost_estimate=pl.CostEstimate(flops=0, bytes_accessed=MIB, transcendentals=0),
        name="merge",
    )(jnp.stack([side, core]).astype(jnp.int32), even, odd, after, before)


def sum_kernel(slots, near, mid, far, crossed, up, down, far_turned, out_ref):
    pairs = (
        (near[0], crossed[0]),
        (near[1], down[0]),
        (mid[0], up[0]),
        (mid[1], down[1]),
        (mid[2], up[1]),
        (far[0], far_turned[...]),
    )
    for k, (one, two) in enumerate(pairs):
        out_ref[slots[k]] = (one.astype(jnp.float32) + two.astype(jnp.float32)).astype(jnp.bfloat16)


def add_up(slots, *parts):
    whole = pl.BlockSpec(memory_space=pltpu.VMEM)
    return pl.pallas_call(
        sum_kernel,
        out_shape=jax.ShapeDtypeStruct((6, B, B), jnp.bfloat16),
        in_specs=[pl.BlockSpec(memory_space=pltpu.SMEM)] + [whole] * len(parts),
        out_specs=whole,
        compiler_params=pltpu.CompilerParams(vmem_limit_bytes=40 * MIB),
        cost_estimate=pl.CostEstimate(flops=6 * B * B, bytes_accessed=9 * MIB, transcendentals=0),
        name="add_up",
    )(slots, *parts)


def local(features, sources):
    me = lax.axis_index("blk")
    odd = me % 2
    place = (me - SEAM_AT) % SEAM
    spot = me % PLANE
    side = jnp.where(spot < 2, 1, jnp.where(spot >= PLANE - 2, 2, 0))
    own_half = ((me - SEAM_AT) % N) // SEAM
    tags = (sources[:, None] == jnp.arange(TAG, dtype=sources.dtype)[None, :]).astype(jnp.bfloat16)
    keep, other, ahead = make_units(features, tags, own_half, ((me - 2 - SEAM_AT) % N) // SEAM)

    def place_of(i):
        return (i - SEAM_AT) % SEAM

    after2 = send(ahead, lambda i: i - 2, lambda i: border_side(i) != 1)
    before2 = send(keep, lambda i: i + 2, lambda i: border_side(i) != 2)
    first, second = border_routes()
    crossed_once = lax.ppermute(keep, "blk", first)
    second_half = send(
        keep,
        lambda i: i - PLANE if place_of(i) == 1 else i + SEAM,
        lambda i: place_of(i) < 3,
    )
    opposite = send(hold(other, crossed_once), lambda i: i + SEAM)
    crossed_twice = lax.ppermute(crossed_once, "blk", second)
    mate = send(hold(keep, after2, before2, opposite, second_half, crossed_twice), lambda i: i ^ 1)
    second_round = send(
        hold(second_half, after2, before2, opposite), lambda i: i - PLANE, lambda i: place_of(i + PLANE) == 1
    )
    edge = jnp.where(place == 2, other, crossed_once)
    after2, before2, mate, edge = lax.optimization_barrier((after2, before2, mate, edge))
    after2, before2 = merge(side, odd, crossed_twice, crossed_once, after2, before2)
    before3 = send(before2, lambda i: i + 1, lambda i: i % 2 == 1 and i % PLANE != PLANE - 1)
    after3 = send(after2, lambda i: i - 1, lambda i: i % 2 == 0 and i % PLANE != 0 and place_of(i) != 0)
    after_mate = send(after2, lambda i: i ^ 1)
    before_mate = send(before2, lambda i: i ^ 1)

    zero = jnp.zeros((), jnp.int32)
    seam = jnp.where(place == 0, 1, jnp.where(place == 1, 2, 0))
    rows = [opposite, second_half, second_round]
    rows = [opposite, second_half, second_round]
    near, turned0, turned1 = tiles(rows[:1], [[mate], [after2]], zero, [zero] * 2, ())
    edge = lax.ppermute(hold(edge, turned1), "blk", edge_routes())
    mid, turned2, crossed = tiles(
        [hold(opposite, near)] + rows[1:],
        [[before2], [after_mate], [before_mate]],
        seam,
        [zero] * 3,
        (0, 2),
        (1, 2),
        True,
    )
    crossed = jnp.concatenate([turned0[None], crossed])
    far_choice = jnp.where((spot == 0) | (spot == PLANE - 1) | (place == SEAM - 1), 2, odd)
    far, far_turned = tiles(
        [hold(opposite, mid), second_half],
        [[before3, after3, edge]],
        jnp.where((odd == 0) & (place < 3), 1, 0),
        [far_choice],
        (0,),
    )

    near = send(near, lambda i: i + SEAM)
    mid = send(mid, lambda i: i + SEAM)
    crossed = hold(crossed, near)
    far = send(far, lambda i: i + SEAM)
    crossed = send(crossed, lambda i: i ^ 1)
    turned1, turned2, crossed = hold(turned1, before3, after3), hold(turned2, before3, after3), crossed
    up = send(jnp.stack([turned1, crossed[1]]), lambda i: i + 2)
    down = send(jnp.stack([turned2, crossed[2]]), lambda i: i - 2)
    far_turned = send(far_turned, lambda i: i + 3 if i % 2 else i - 3)
    slots = jnp.where(odd == 1, jnp.array([4, 3, 2, 5, 0, 1], jnp.int32), jnp.array([5, 3, 2, 1, 4, 0], jnp.int32))
    return jnp.transpose(add_up(slots, near, mid, far, crossed, up, down, far_turned), (1, 0, 2))


def solution(mesh):
    return jax.shard_map(
        local,
        mesh=mesh,
        in_specs=(P("blk", None), P("blk")),
        out_specs=P("blk", None, None),
        check_vma=False,
    )
```
